32 devices in a mesh: fg: 4 (over y, core), sp: 8 (over z, x).
Axes of the slice: x: 2, y: 2, z: 4, core: 2. Of those that a mesh axis runs over, the one named last changes fastest.
Arguments:
- latent: bfloat16 [16, 64, 240, 256], P('fg', 'sp'), may hold values from -6 to 6
- temporal_weight: bfloat16 [3, 256, 1024], replicated, may hold values from -0.21875 to 0.21875
- temporal_bias: float32 [1024], replicated, may hold values from -4 to 4
- spatial_weight: bfloat16 [3, 3, 256, 128], replicated, may hold values from -0.125 to 0.125
- spatial_bias: float32 [128], replicated, may hold values from -4 to 4
- counts: int32 [4], replicated, may hold values from 1 to 16, 48 in all
Outputs:
- decoded: bfloat16 [64, 64, 240, 128], P('fg', 'sp')
The draws below stay inside these ranges and needn't reach their ends.
Inputs may be any that keep to these rules, and one draw needn't show every extreme that they name: `counts`: some group holds 16.
All inputs are finite; a program needn't handle non-finite values.
Results may differ from the reference program's by a relative error of at most 0.0038.
Values may be sent and summed in bfloat16 or wider, within the bound.
A program may use at most 320 MiB of HBM per device.

```python
import math
import jax
import jax.numpy as jnp
import numpy as np
from jax import lax

CT = 256
CS = 128
W = 240
LF = 4
LATENT = 16
FRAMES = 64
H = 64
N_FG = 4


def block_scale(key, dims, cuts, least, largest):
    def one(axis_at, parts):
        heights = jax.random.uniform(jax.random.fold_in(jax.random.fold_in(key, 6), axis_at), (parts,), jnp.float32, least / len(cuts), largest / len(cuts))
        return jnp.repeat(jnp.exp(heights), dims[axis_at] // parts).reshape((-1,) + (1,) * (len(dims) - axis_at - 1))

    gain = one(*cuts[0])
    for cut in cuts[1:]:
        gain = gain * one(*cut)
    return gain


def split_up(amount, total, limit, lean):
    portions = [(1 << 20) // math.isqrt(standing ** lean) + 1 for standing in range(2, amount + 1)]
    rest, given = total - limit - (amount - 1), [1] * (amount - 1)
    while rest > 0:
        free = [i for i in range(amount - 1) if given[i] < limit]
        pool, budget = sum([portions[i] for i in free]), rest
        for i in free:
            more = min(limit - given[i], max(1, budget * portions[i] // pool), rest)
            given[i] = given[i] + more
            rest = rest - more
    return np.array([limit] + given)


def ragged(key, number_of, total, limit, lean):
    if number_of == 2:
        one = jax.random.randint(key, (), max(1, total - limit), min(limit, total - 1) + 1)
        return jnp.stack([one, total - one])
    tallies = jnp.asarray(split_up(number_of, total, limit, lean), jnp.int32)
    twos = (number_of - 1) // 2
    source_of, sink = tallies[1:1 + 2 * twos:2], tallies[2:2 + 2 * twos:2]
    room = jnp.minimum(source_of - 1, limit - sink)
    shifted = jax.random.randint(jax.random.fold_in(key, 1), (twos,), 0, 1 << 20) % (room + 1)
    tallies = tallies.at[1:1 + 2 * twos:2].set(source_of - shifted).at[2:2 + 2 * twos:2].set(sink + shifted)
    return tallies[jax.random.permutation(jax.random.fold_in(key, 2), number_of)]


def bell_draw(key, shape, width, most, shards=(), held_as=jnp.bfloat16):
    values = width * jax.random.normal(key, shape, jnp.float32)
    if shards:
        values = values * block_scale(key, shape, shards, -0.22, 0.18)
    return jnp.clip(values, -most, most).astype(held_as)


def setup_inputs(seed: int = 0) -> dict:
    arg_keys = jax.random.split(jax.random.key(seed), 7)
    return {
        "latent": bell_draw(arg_keys[0], (LATENT, H, W, CT), 1.0, 6.0, ((0, 4), (1, 8))),
        "temporal_weight": bell_draw(arg_keys[1], (3, CT, 4 * CT), (3 * CT) ** -0.5, 0.21875),
        "temporal_bias": bell_draw(arg_keys[2], (4 * CT,), 1.0, 4.0, (), jnp.float32),
        "spatial_weight": bell_draw(arg_keys[3], (3, 3, CT, CS), (9 * CT) ** -0.5, 0.125),
        "spatial_bias": bell_draw(arg_keys[4], (CS,), 1.0, 4.0, (), jnp.float32),
        "counts": ragged(arg_keys[5], N_FG, 3 * LF * N_FG, 4 * LF, 1).astype(jnp.int32),
    }


def reference(latent, temporal_weight, temporal_bias, spatial_weight, spatial_bias, counts):
    zeros = jnp.zeros((2,) + latent.shape[1:], jnp.bfloat16)
    padded = jnp.concatenate([zeros, latent], axis=0)
    kernel = temporal_weight.astype(jnp.float32).reshape(3, CT, 4, CT)
    bias_t = temporal_bias.reshape(4, 1, 1, CT)
    swf = spatial_weight.astype(jnp.float32)

    def one_frame(index):
        window = lax.dynamic_slice_in_dim(padded, index, 3, 0).astype(jnp.float32)
        pre = jnp.einsum("khwc,kcjd->jhwd", window, kernel) + bias_t
        upper = jax.nn.silu(pre).astype(jnp.bfloat16)
        framed = jnp.pad(upper, ((0, 0), (1, 1), (1, 1), (0, 0))).astype(jnp.float32)
        total = jnp.zeros((4, H, W, CS), jnp.float32)
        for dy in range(3):
            for dx in range(3):
                total = total + jnp.einsum("fhwc,cd->fhwd", framed[:, dy:dy + H, dx:dx + W, :], swf[dy, dx])
        out = (total + spatial_bias).astype(jnp.bfloat16)
        frame_ids = 4 * index + jnp.arange(4, dtype=jnp.int32)
        group = frame_ids // (4 * LF)
        valid = (frame_ids % (4 * LF)) < counts[group]
        return out * valid.astype(jnp.bfloat16).reshape(4, 1, 1, 1)

    result = lax.map(one_frame, jnp.arange(LATENT, dtype=jnp.int32))
    return result.reshape(FRAMES, H, W, CS)
```

```python
import functools

import jax
import jax.numpy as jnp
from jax import lax
from jax.experimental import pallas as pl
from jax.experimental.pallas import tpu as pltpu
from jax.sharding import PartitionSpec as P

F32, BF16 = jnp.float32, jnp.bfloat16
LIMIT = 46 * 1024 * 1024
MESH = pl.DeviceIdType.MESH
SENDS = ((0, 1), (0, -1), (1, 0), (1, 0), (1, 0), (1, 0))
NEIGHBOURS = ((0, 1), (0, -1), (1, 0), (-1, 0))


def silu(pre):
    half = 0.5 * pre
    return half + half * jnp.tanh(half)


def fill_weights(sw_ref, w01, w2):
    depth, wide = sw_ref.shape[2], sw_ref.shape[3]
    zero = jnp.zeros((depth, wide), BF16)
    for dy in range(3):
        at = pl.ds(dy * depth, depth)
        w01[at, :wide] = sw_ref[dy, 0]
        w01[at, wide:] = sw_ref[dy, 1]
    for q in range(4):
        at = pl.ds(q * depth, depth)
        w2[at, :wide] = sw_ref[q, 2] if q < 3 else zero
        w2[at, wide:] = sw_ref[q - 1, 2] if q > 0 else zero


def activation(a, j, tw_ref, tb_ref):
    width = tw_ref.shape[1] // 4
    columns = pl.ds(pl.multiple_of(j * width, width), width)
    pre = jnp.dot(a, tw_ref[:, columns], preferred_element_type=F32) + tb_ref[:, columns]
    return silu(pre).astype(BF16)


def zero_rims(left, right, cols):
    n, _, wide = left.shape
    left[:, 0:8, :] = jnp.zeros((n, 8, wide), F32)
    right[:, cols:cols + 8, :] = jnp.zeros((n, 8, wide), F32)


def row_pair(row, cols, w01, w2, left, mid, right, sb_ref, p):
    wide = sb_ref.shape[1]
    taps = [row(q) for q in range(4)]
    a = jnp.concatenate([jnp.concatenate(taps[h:h + 3], axis=1) for h in range(2)], axis=0)
    r = jnp.dot(a, w01[...], preferred_element_type=F32)
    s = jnp.dot(jnp.concatenate(taps, axis=1), w2[...], preferred_element_type=F32)
    rows = []
    for h in range(2):
        left[2 * p + h, 8:8 + cols, :] = r[h * cols:(h + 1) * cols, :wide]
        right[2 * p + h, 0:cols, :] = s[:, h * wide:(h + 1) * wide]
        mid[2 * p + h] = r[h * cols:(h + 1) * cols, wide:]
        total = left[2 * p + h, 7:7 + cols, :] + mid[2 * p + h] + right[2 * p + h, 1:1 + cols, :] + sb_ref[...]
        rows.append(total.astype(BF16))
    return rows


def frames_kernel(sizes, latent_ref, tw_ref, tb_ref, sw_ref, sb_ref, out_ref,
                  x, halo, up, tw, sw, w01, w2, w3, left, mid, right, load_sem, send_sem, recv_sem):
    frames, rows, cols, width = latent_ref.shape
    wide = sb_ref.shape[1]
    fg, sp = lax.axis_index("fg"), lax.axis_index("sp")
    last_fg, last_sp = sizes[0] - 1, sizes[1] - 1

    def there(by, back=False):
        f, s = (fg - by[0], sp - by[1]) if back else (fg + by[0], sp + by[1])
        return (f >= 0) & (f <= last_fg) & (s >= 0) & (s <= last_sp)

    barrier = pltpu.get_barrier_semaphore()
    for by in NEIGHBOURS:
        @pl.when(there(by))
        def _():
            pl.semaphore_signal(barrier, inc=1, device_id=(fg + by[0], sp + by[1]), device_id_type=MESH)

    loads = [pltpu.make_async_copy(latent_ref.at[f], x.at[2 + f], load_sem.at[f]) for f in range(frames)]
    loads.append(pltpu.make_async_copy(tw_ref, tw, load_sem.at[frames]))
    loads.append(pltpu.make_async_copy(sw_ref, sw, load_sem.at[frames + 1]))
    for load in loads:
        load.start()

    near = [(at > 0).astype(jnp.int32) + (at < n).astype(jnp.int32) for at, n in ((fg, last_fg), (sp, last_sp))]
    pl.semaphore_wait(barrier, near[0] + near[1])

    own, tail, before = pl.ds(2, frames), pl.ds(frames, 2), pl.ds(0, 2)
    sources = (latent_ref.at[:, rows - 1], latent_ref.at[:, 0], latent_ref.at[frames - 1], latent_ref.at[frames - 2],
               halo.at[0, tail], halo.at[1, tail])
    targets = (halo.at[0, own], halo.at[1, own], x.at[1], x.at[0], halo.at[0, before], halo.at[1, before])

    def sent(i):
        by = SENDS[i]
        return pltpu.make_async_remote_copy(
            src_ref=sources[i], dst_ref=targets[i], send_sem=send_sem.at[i], recv_sem=recv_sem.at[i],
            device_id=(fg + by[0], sp + by[1]), device_id_type=MESH,
        )

    above, below = sp > 0, sp < last_sp
    sends = [there(by) for by in SENDS[:4]] + [(fg < last_fg) & above, (fg < last_fg) & below]
    arrives = [there(by, True) for by in SENDS[:4]] + [(fg > 0) & above, (fg > 0) & below]

    def start(*which):
        for i in which:
            @pl.when(sends[i])
            def _():
                sent(i).start()

    def arrived(*which):
        for i in which:
            @pl.when(arrives[i])
            def _():
                sent(i).wait_recv()

    start(0, 1, 2, 3)

    @pl.when(fg == 0)
    def _():
        x[0:2] = jnp.zeros((2, rows, cols, width), BF16)
        halo[:, 0:2] = jnp.zeros((2, 2, cols, width), BF16)

    for side, there_is in enumerate((above, below)):
        @pl.when(jnp.logical_not(there_is))
        def _():
            halo[side] = jnp.zeros((frames + 2, cols, width), BF16)

    zero_rims(left, right, cols)
    for load in loads[::-1]:
        load.wait()
    fill_weights(sw, w01, w2)
    for dy in range(3):
        for dx in range(3):
            w3[dy * width:(dy + 1) * width, dx * wide:(dx + 1) * wide] = sw[dy, dx]

    def inner(i, carry):
        l, j = i // 4, i % 4
        for t in range(0, rows, 2):
            a = jnp.concatenate([x[l + k, t:t + 2].reshape(2 * cols, width) for k in range(3)], axis=1)
            up[i, t * cols:(t + 2) * cols, :] = activation(a, j, tw, tb_ref)
        for p in range(rows // 2 - 1):
            row = lambda q: up[i, pl.ds((2 * p + q) * cols, cols), :]
            for h, value in enumerate(row_pair(row, cols, w01, w2, left, mid, right, sb_ref, p)):
                out_ref[i, 2 * p + 1 + h] = value
        return carry

    def rim(i, carry):
        l, j = i // 4, i % 4
        a = jnp.concatenate([halo[:, l + k].reshape(2 * cols, width) for k in range(3)], axis=1)
        act = activation(a, j, tw, tb_ref)
        zero = jnp.zeros((cols, width), BF16)
        row = lambda h: up[i, pl.ds(h * cols, cols), :]
        first = [jnp.where(above, act[:cols], zero), row(0), row(1)]
        final = [row(rows - 2), row(rows - 1), jnp.where(below, act[cols:], zero)]
        a = jnp.concatenate([jnp.concatenate(first, axis=1), jnp.concatenate(final, axis=1)], axis=0)
        r = jnp.dot(a, w3[...], preferred_element_type=F32)
        for h in range(2):
            part = r[h * cols:(h + 1) * cols]
            left[h, 8:8 + cols, :] = part[:, :wide]
            right[h, 0:cols, :] = part[:, 2 * wide:]
            total = left[h, 7:7 + cols, :] + (part[:, wide:2 * wide] + sb_ref[...]) + right[h, 1:1 + cols, :]
            out_ref[i, h * (rows - 1)] = total.astype(BF16)
        return carry

    lax.fori_loop(8, 16, inner, 0)
    arrived(2)
    lax.fori_loop(4, 8, inner, 0)
    arrived(0, 1)
    start(4, 5)
    lax.fori_loop(8, 16, rim, 0)
    arrived(3)
    lax.fori_loop(0, 4, inner, 0)
    arrived(4, 5)
    lax.fori_loop(0, 8, rim, 0)

    for i in range(len(SENDS)):
        @pl.when(sends[i])
        def _():
            sent(i).wait_send()


def frames_call(sizes, latent, tw, tb, sw, sb):
    frames, rows, cols, width = latent.shape
    wide = sw.shape[3]
    vmem = pl.BlockSpec(memory_space=pltpu.VMEM)
    hbm = pl.BlockSpec(memory_space=pl.ANY)
    return pl.pallas_call(
        functools.partial(frames_kernel, sizes),
        in_specs=[hbm, hbm, vmem, hbm, vmem],
        out_specs=vmem,
        out_shape=pltpu.VMEM((4 * frames, rows, cols, wide), BF16),
        scratch_shapes=[
            pltpu.VMEM((frames + 2, rows, cols, width), BF16),
            pltpu.VMEM((2, frames + 2, cols, width), BF16),
            pltpu.VMEM((4 * frames, rows * cols, width), BF16),
            pltpu.VMEM(tw.shape, BF16),
            pltpu.VMEM(sw.shape, BF16),
            pltpu.VMEM((3 * width, 2 * wide), BF16),
            pltpu.VMEM((4 * width, 2 * wide), BF16),
            pltpu.VMEM((3 * width, 3 * wide), BF16),
            pltpu.VMEM((rows, cols + 8, wide), F32),
            pltpu.VMEM((rows, cols, wide), F32),
            pltpu.VMEM((rows, cols + 8, wide), F32),
            pltpu.SemaphoreType.DMA((frames + 2,)),
            pltpu.SemaphoreType.DMA((len(SENDS),)),
            pltpu.SemaphoreType.DMA((len(SENDS),)),
        ],
        compiler_params=pltpu.CompilerParams(
            collective_id=0, has_side_effects=True, vmem_limit_bytes=LIMIT
        ),
        cost_estimate=pl.CostEstimate(flops=36 * 10**9, bytes_accessed=16 * 10**6, transcendentals=10**7),
        name="frames",
    )(latent, tw, tb, sw, sb)


def flush_kernel(counts_ref, decoded_ref, out_ref, zero, sem):
    limit = counts_ref[lax.axis_index("fg")]
    zero[...] = jnp.zeros(zero.shape, BF16)
    count = decoded_ref.shape[0]
    copies = [pltpu.make_async_copy(decoded_ref.at[f], out_ref.at[f], sem.at[f]) for f in range(count)]
    for f, copy in enumerate(copies):
        pl.when(f < limit)(copy.start)
        pl.when(f >= limit)(pltpu.make_async_copy(zero, out_ref.at[f], sem.at[f]).start)
    for copy in copies:
        copy.wait()


def flush_call(counts, decoded):
    return pl.pallas_call(
        flush_kernel,
        in_specs=[pl.BlockSpec(memory_space=pltpu.SMEM), pl.BlockSpec(memory_space=pltpu.VMEM)],
        out_specs=pl.BlockSpec(memory_space=pl.ANY),
        out_shape=jax.ShapeDtypeStruct(decoded.shape, BF16),
        scratch_shapes=[pltpu.VMEM(decoded.shape[1:], BF16), pltpu.SemaphoreType.DMA((decoded.shape[0],))],
        compiler_params=pltpu.CompilerParams(vmem_limit_bytes=16 * 1024 * 1024),
        cost_estimate=pl.CostEstimate(flops=0, bytes_accessed=16 * 10**6, transcendentals=0),
        name="flush",
    )(counts, decoded)


def on_device(sizes, latent, temporal_weight, temporal_bias, spatial_weight, spatial_bias, counts):
    width = latent.shape[3]
    tw = temporal_weight.reshape(3 * width, 4 * width)
    args = (tw, temporal_bias.reshape(1, -1), spatial_weight, spatial_bias.reshape(1, -1))
    return flush_call(counts, frames_call(sizes, latent, *args))


def solution(mesh):
    sizes = (mesh.shape["fg"], mesh.shape["sp"])
    return jax.shard_map(
        functools.partial(on_device, sizes),
        mesh=mesh,
        in_specs=(P("fg", "sp", None, None), P(), P(), P(), P(), P()),
        out_specs=P("fg", "sp", None, None),
        check_vma=False,
    )
```

```python
import functools

import jax
import jax.numpy as jnp
from jax import lax
from jax.experimental import pallas as pl
from jax.experimental.pallas import tpu as pltpu
from jax.sharding import PartitionSpec as P

F32, BF16 = jnp.float32, jnp.bfloat16
LIMIT = 40 * 1024 * 1024
MESH = pl.DeviceIdType.MESH
SENDS = ((0, 1), (0, -1)) + ((1, 0),) * 6
NEIGHBOURS = ((0, 1), (0, -1), (1, 0), (-1, 0))


def silu(pre):
    half = 0.5 * pre
    return half + half * jnp.tanh(half)


def fill_weights(sw_ref, w01, w2):
    depth, wide = sw_ref.shape[2], sw_ref.shape[3]
    zero = jnp.zeros((depth, wide), BF16)
    for dy in range(3):
        at = pl.ds(dy * depth, depth)
        w01[at, :wide] = sw_ref[dy, 0]
        w01[at, wide:] = sw_ref[dy, 1]
    for q in range(4):
        at = pl.ds(q * depth, depth)
        w2[at, :wide] = sw_ref[q, 2] if q < 3 else zero
        w2[at, wide:] = sw_ref[q - 1, 2] if q > 0 else zero


def activation(a, j, tw_ref, tb_ref):
    width = tw_ref.shape[1] // 4
    columns = pl.ds(pl.multiple_of(j * width, width), width)
    pre = jnp.dot(a, tw_ref[:, columns], preferred_element_type=F32) + tb_ref[:, columns]
    return silu(pre).astype(BF16)


def zero_rims(left, right, cols):
    n, _, wide = left.shape
    left[:, 0:8, :] = jnp.zeros((n, 8, wide), F32)
    right[:, cols:cols + 8, :] = jnp.zeros((n, 8, wide), F32)


def row_pair(row, cols, w01, w2, left, mid, right, sb_ref, p):
    wide = sb_ref.shape[1]
    taps = [row(q) for q in range(4)]
    a = jnp.concatenate([jnp.concatenate(taps[h:h + 3], axis=1) for h in range(2)], axis=0)
    r = jnp.dot(a, w01[...], preferred_element_type=F32)
    s = jnp.dot(jnp.concatenate(taps, axis=1), w2[...], preferred_element_type=F32)
    rows = []
    for h in range(2):
        left[2 * p + h, 8:8 + cols, :] = r[h * cols:(h + 1) * cols, :wide]
        right[2 * p + h, 0:cols, :] = s[:, h * wide:(h + 1) * wide]
        mid[2 * p + h] = r[h * cols:(h + 1) * cols, wide:]
        total = left[2 * p + h, 7:7 + cols, :] + mid[2 * p + h] + right[2 * p + h, 1:1 + cols, :] + sb_ref[...]
        rows.append(total.astype(BF16))
    return rows


def frames_kernel(sizes, latent_ref, tw_ref, tb_ref, sw_ref, sb_ref,
                  out_ref, x, halo, tw, tb, sb, w01, w2,
                  up, sw, w3, left, mid, right, load_sem, send_sem, recv_sem):
    frames, rows, cols, width = latent_ref.shape
    wide = sb_ref.shape[1]
    fg, sp = lax.axis_index("fg"), lax.axis_index("sp")
    last_fg, last_sp = sizes[0] - 1, sizes[1] - 1

    def there(by, back=False):
        f, s = (fg - by[0], sp - by[1]) if back else (fg + by[0], sp + by[1])
        return (f >= 0) & (f <= last_fg) & (s >= 0) & (s <= last_sp)

    barrier = pltpu.get_barrier_semaphore()
    for by in NEIGHBOURS:
        @pl.when(there(by))
        def _():
            pl.semaphore_signal(barrier, inc=1, device_id=(fg + by[0], sp + by[1]), device_id_type=MESH)

    moves = [(sw_ref, sw), (tw_ref, tw), (tb_ref, tb), (sb_ref, sb)]
    moves += [(latent_ref.at[f], x.at[2 + f]) for f in range(frames)]
    loads = [pltpu.make_async_copy(source, target, load_sem.at[n]) for n, (source, target) in enumerate(moves)]
    for load in loads:
        load.start()

    zero_rims(left, right, cols)
    loads[0].wait()
    fill_weights(sw, w01, w2)
    for dy in range(3):
        for dx in range(3):
            w3[dy * width:(dy + 1) * width, dx * wide:(dx + 1) * wide] = sw[dy, dx]

    near = [(at > 0).astype(jnp.int32) + (at < n).astype(jnp.int32) for at, n in ((fg, last_fg), (sp, last_sp))]
    pl.semaphore_wait(barrier, near[0] + near[1])

    own = pl.ds(2, frames)
    sources = [latent_ref.at[:, rows - 1], latent_ref.at[:, 0], latent_ref.at[frames - 1], latent_ref.at[frames - 2]]
    targets = [halo.at[0, own], halo.at[1, own], x.at[1], x.at[0]]
    for k in (1, 0):
        sources += [halo.at[side, frames + k] for side in range(2)]
        targets += [halo.at[side, k] for side in range(2)]

    def sent(i):
        by = SENDS[i]
        return pltpu.make_async_remote_copy(
            src_ref=sources[i], dst_ref=targets[i], send_sem=send_sem.at[i], recv_sem=recv_sem.at[i],
            device_id=(fg + by[0], sp + by[1]), device_id_type=MESH,
        )

    above, below = sp > 0, sp < last_sp
    sends = [there(by) for by in SENDS[:4]] + [(fg < last_fg) & side for side in (above, below)] * 2
    arrives = [there(by, True) for by in SENDS[:4]] + [(fg > 0) & side for side in (above, below)] * 2

    def start(*which):
        for i in which:
            @pl.when(sends[i])
            def _():
                sent(i).start()

    def arrived(*which):
        for i in which:
            @pl.when(arrives[i])
            def _():
                sent(i).wait_recv()

    start(0, 1, 2, 3)

    @pl.when(fg == 0)
    def _():
        x[0:2] = jnp.zeros((2, rows, cols, width), BF16)
        halo[:, 0:2] = jnp.zeros((2, 2, cols, width), BF16)

    for side, there_is in enumerate((above, below)):
        @pl.when(jnp.logical_not(there_is))
        def _():
            halo[side] = jnp.zeros((frames + 2, cols, width), BF16)

    for load in loads[1:]:
        load.wait()

    def inner(n, carry):
        l = frames - 1 - n

        @pl.when(l == 1)
        def _():
            arrived(2)

        for j in range(4):
            i = 4 * l + j - 4
            for t in range(0, rows, 2):
                a = jnp.concatenate([x[l + k, t:t + 2].reshape(2 * cols, width) for k in range(3)], axis=1)
                up[i, t * cols:(t + 2) * cols, :] = activation(a, j, tw, tb)
            for p in range(rows // 2 - 1):
                row = lambda q: up[i, pl.ds((2 * p + q) * cols, cols), :]
                for h, value in enumerate(row_pair(row, cols, w01, w2, left, mid, right, sb, p)):
                    out_ref[i, 2 * p + 1 + h] = value
        return carry

    def rim(n, carry):
        l = frames - 1 - n

        @pl.when(l == 1)
        def _():
            arrived(4, 5)

        for j in range(4):
            i = 4 * l + j - 4
            a = jnp.concatenate([halo[:, l + k].reshape(2 * cols, width) for k in range(3)], axis=1)
            act = activation(a, j, tw, tb)
            zero = jnp.zeros((cols, width), BF16)
            row = lambda h: up[i, pl.ds(h * cols, cols), :]
            first = [jnp.where(above, act[:cols], zero), row(0), row(1)]
            final = [row(rows - 2), row(rows - 1), jnp.where(below, act[cols:], zero)]
            a = jnp.concatenate([jnp.concatenate(first, axis=1), jnp.concatenate(final, axis=1)], axis=0)
            r = jnp.dot(a, w3[...], preferred_element_type=F32)
            for h in range(2):
                part = r[h * cols:(h + 1) * cols]
                left[h, 8:8 + cols, :] = part[:, :wide]
                right[h, 0:cols, :] = part[:, 2 * wide:]
                total = left[h, 7:7 + cols, :] + (part[:, wide:2 * wide] + sb[...]) + right[h, 1:1 + cols, :]
                out_ref[i, h * (rows - 1)] = total.astype(BF16)
        return carry

    lax.fori_loop(0, frames - 1, inner, 0)
    arrived(0, 1)
    start(4, 5, 6, 7)
    lax.fori_loop(0, frames - 1, rim, 0)
    arrived(3, 6, 7)

    for i in range(len(SENDS)):
        @pl.when(sends[i])
        def _():
            sent(i).wait_send()


def frames_call(sizes, latent, tw, tb, sw, sb):
    frames, rows, cols, width = latent.shape
    wide = sw.shape[3]
    vmem = pl.BlockSpec(memory_space=pltpu.VMEM)
    hbm = pl.BlockSpec(memory_space=pl.ANY)
    out_shape = [
        pltpu.VMEM((4 * frames - 4, rows, cols, wide), BF16),
        pltpu.VMEM((frames + 2, rows, cols, width), BF16),
        pltpu.VMEM((2, frames + 2, cols, width), BF16),
        pltpu.VMEM(tw.shape, BF16),
        pltpu.VMEM(tb.shape, F32),
        pltpu.VMEM(sb.shape, F32),
        pltpu.VMEM((3 * width, 2 * wide), BF16),
        pltpu.VMEM((4 * width, 2 * wide), BF16),
    ]
    return pl.pallas_call(
        functools.partial(frames_kernel, sizes),
        in_specs=[hbm] * 5,
        out_specs=[vmem] * len(out_shape),
        out_shape=out_shape,
        scratch_shapes=[
            pltpu.VMEM((4 * frames - 4, rows * cols, width), BF16),
            pltpu.VMEM(sw.shape, BF16),
            pltpu.VMEM((3 * width, 3 * wide), BF16),
            pltpu.VMEM((rows, cols + 8, wide), F32),
            pltpu.VMEM((rows, cols, wide), F32),
            pltpu.VMEM((rows, cols + 8, wide), F32),
            pltpu.SemaphoreType.DMA((frames + 4,)),
            pltpu.SemaphoreType.DMA((len(SENDS),)),
            pltpu.SemaphoreType.DMA((len(SENDS),)),
        ],
        compiler_params=pltpu.CompilerParams(
            collective_id=0, has_side_effects=True, vmem_limit_bytes=LIMIT
        ),
        cost_estimate=pl.CostEstimate(flops=28 * 10**9, bytes_accessed=16 * 10**6, transcendentals=10**7),
        name="frames",
    )(latent, tw, tb, sw, sb)


def finish_kernel(counts_ref, late_ref, x, halo, tw, tb, sb, w01, w2, out_ref,
                  early, zero, up, left, mid, right, sem):
    rows, cols, width = x.shape[1:]
    fg, sp = lax.axis_index("fg"), lax.axis_index("sp")
    last_sp = lax.axis_size("sp") - 1
    limit = counts_ref[fg]
    zero[...] = jnp.zeros(zero.shape, BF16)

    def copy(source, f):
        return pltpu.make_async_copy(source, out_ref.at[f], sem.at[f])

    def leave(source, f):
        pl.when(f < limit)(copy(source, f).start)
        pl.when(f >= limit)(copy(zero, f).start)

    late = late_ref.shape[0]
    for f in range(late):
        leave(late_ref.at[f], 4 + f)
    zero_rims(left, right, cols)

    def rows_of(t, k):
        if t == 0:
            return jnp.concatenate([halo[0, k], x[k, 0]], axis=0)
        if t == rows:
            return jnp.concatenate([x[k, rows - 1], halo[1, k]], axis=0)
        return x[k, t - 1:t + 1].reshape(2 * cols, width)

    for j in range(4):
        for t in range(0, rows + 2, 2):
            a = jnp.concatenate([rows_of(t, k) for k in range(3)], axis=1)
            up[j, t * cols:(t + 2) * cols, :] = activation(a, j, tw, tb)

        @pl.when(sp == 0)
        def _():
            up[j, 0:cols, :] = jnp.zeros((cols, width), BF16)

        @pl.when(sp == last_sp)
        def _():
            up[j, (rows + 1) * cols:, :] = jnp.zeros((cols, width), BF16)

        for p in range(rows // 2):
            row = lambda q: up[j, pl.ds((2 * p + q) * cols, cols), :]
            for h, value in enumerate(row_pair(row, cols, w01, w2, left, mid, right, sb, p)):
                early[j, 2 * p + h] = value
        leave(early.at[j], j)

    for f in range(late + 4):
        copy(zero, f).wait()


def finish_call(counts, late, x, *args):
    _, rows, cols, wide = late.shape
    width = x.shape[3]
    shape = (late.shape[0] + 4, rows, cols, wide)
    vmem = pl.BlockSpec(memory_space=pltpu.VMEM)
    return pl.pallas_call(
        finish_kernel,
        in_specs=[pl.BlockSpec(memory_space=pltpu.SMEM)] + [vmem] * (2 + len(args)),
        out_specs=pl.BlockSpec(memory_space=pl.ANY),
        out_shape=jax.ShapeDtypeStruct(shape, BF16),
        scratch_shapes=[
            pltpu.VMEM((4,) + shape[1:], BF16),
            pltpu.VMEM(shape[1:], BF16),
            pltpu.VMEM((4, (rows + 2) * cols, width), BF16),
            pltpu.VMEM((rows, cols + 8, wide), F32),
            pltpu.VMEM((rows, cols, wide), F32),
            pltpu.VMEM((rows, cols + 8, wide), F32),
            pltpu.SemaphoreType.DMA((shape[0],)),
        ],
        compiler_params=pltpu.CompilerParams(vmem_limit_bytes=24 * 1024 * 1024),
        cost_estimate=pl.CostEstimate(flops=9 * 10**9, bytes_accessed=16 * 10**6, transcendentals=10**6),
        name="finish",
    )(counts, late, x, *args)


def on_device(sizes, latent, temporal_weight, temporal_bias, spatial_weight, spatial_bias, counts):
    width = latent.shape[3]
    tw = temporal_weight.reshape(3 * width, 4 * width)
    args = (tw, temporal_bias.reshape(1, -1), spatial_weight, spatial_bias.reshape(1, -1))
    return finish_call(counts, *frames_call(sizes, latent, *args))


def solution(mesh):
    sizes = (mesh.shape["fg"], mesh.shape["sp"])
    return jax.shard_map(
        functools.partial(on_device, sizes),
        mesh=mesh,
        in_specs=(P("fg", "sp", None, None), P(), P(), P(), P(), P()),
        out_specs=P("fg", "sp", None, None),
        check_vma=False,
    )
```

```python
import functools

import jax
import jax.numpy as jnp
from jax import lax
from jax.experimental import pallas as pl
from jax.experimental.pallas import tpu as pltpu
from jax.sharding import PartitionSpec as P

F32, BF16 = jnp.float32, jnp.bfloat16
LIMIT = 40 * 1024 * 1024
MESH = pl.DeviceIdType.MESH
SENDS = ((0, 1), (0, -1)) + ((1, 0),) * 6
NEIGHBOURS = ((0, 1), (0, -1), (1, 0), (-1, 0))


def silu(pre):
    half = 0.5 * pre
    return half + half * jnp.tanh(half)


def fill_weights(sw_ref, w01, w2):
    depth, wide = sw_ref.shape[2], sw_ref.shape[3]
    zero = jnp.zeros((depth, wide), BF16)
    for dy in range(3):
        at = pl.ds(dy * depth, depth)
        w01[at, :wide] = sw_ref[dy, 0]
        w01[at, wide:] = sw_ref[dy, 1]
    for q in range(4):
        at = pl.ds(q * depth, depth)
        w2[at, :wide] = sw_ref[q, 2] if q < 3 else zero
        w2[at, wide:] = sw_ref[q - 1, 2] if q > 0 else zero


def activation(a, j, tw_ref, tb_ref):
    width = tw_ref.shape[1] // 4
    columns = pl.ds(pl.multiple_of(j * width, width), width)
    pre = jnp.dot(a, tw_ref[:, columns], preferred_element_type=F32) + tb_ref[:, columns]
    return silu(pre).astype(BF16)


def zero_rims(left, right, cols):
    n, _, wide = left.shape
    left[:, 0:8, :] = jnp.zeros((n, 8, wide), F32)
    right[:, cols:cols + 8, :] = jnp.zeros((n, 8, wide), F32)


def row_pair(row, cols, w01, w2, left, mid, right, sb_ref, p):
    wide = sb_ref.shape[1]
    taps = [row(q) for q in range(4)]
    a = jnp.concatenate([jnp.concatenate(taps[h:h + 3], axis=1) for h in range(2)], axis=0)
    r = jnp.dot(a, w01[...], preferred_element_type=F32)
    s = jnp.dot(jnp.concatenate(taps, axis=1), w2[...], preferred_element_type=F32)
    rows = []
    for h in range(2):
        left[2 * p + h, 8:8 + cols, :] = r[h * cols:(h + 1) * cols, :wide]
        right[2 * p + h, 0:cols, :] = s[:, h * wide:(h + 1) * wide]
        mid[2 * p + h] = r[h * cols:(h + 1) * cols, wide:]
        total = left[2 * p + h, 7:7 + cols, :] + mid[2 * p + h] + right[2 * p + h, 1:1 + cols, :] + sb_ref[...]
        rows.append(total.astype(BF16))
    return rows


def frames_kernel(sizes, latent_ref, tw_ref, tb_ref, sw_ref, sb_ref,
                  out_ref, x, halo, tw, tb, sb, w01, w2,
                  up, sw, w3, left, mid, right, load_sem, send_sem, recv_sem):
    frames, rows, cols, width = latent_ref.shape
    wide = sb_ref.shape[1]
    fg, sp = lax.axis_index("fg"), lax.axis_index("sp")
    last_fg, last_sp = sizes[0] - 1, sizes[1] - 1

    def there(by, back=False):
        f, s = (fg - by[0], sp - by[1]) if back else (fg + by[0], sp + by[1])
        return (f >= 0) & (f <= last_fg) & (s >= 0) & (s <= last_sp)

    barrier = pltpu.get_barrier_semaphore()
    for by in NEIGHBOURS:
        @pl.when(there(by))
        def _():
            pl.semaphore_signal(barrier, inc=1, device_id=(fg + by[0], sp + by[1]), device_id_type=MESH)

    moves = [(sw_ref, sw), (tw_ref, tw), (tb_ref, tb), (sb_ref, sb)]
    moves += [(latent_ref.at[f], x.at[2 + f]) for f in range(frames)]
    loads = [pltpu.make_async_copy(source, target, load_sem.at[n]) for n, (source, target) in enumerate(moves)]
    for load in loads:
        load.start()

    out_ref[4 * frames - 4] = jnp.zeros(out_ref.shape[1:], BF16)
    zero_rims(left, right, cols)
    loads[0].wait()
    fill_weights(sw, w01, w2)
    for dy in range(3):
        for dx in range(3):
            w3[dy * width:(dy + 1) * width, dx * wide:(dx + 1) * wide] = sw[dy, dx]

    near = [(at > 0).astype(jnp.int32) + (at < n).astype(jnp.int32) for at, n in ((fg, last_fg), (sp, last_sp))]
    pl.semaphore_wait(barrier, near[0] + near[1])

    own = pl.ds(2, frames)
    sources = [latent_ref.at[:, rows - 1], latent_ref.at[:, 0], latent_ref.at[frames - 1], latent_ref.at[frames - 2]]
    targets = [halo.at[0, own], halo.at[1, own], x.at[1], x.at[0]]
    for k in (1, 0):
        sources += [halo.at[side, frames + k] for side in range(2)]
        targets += [halo.at[side, k] for side in range(2)]

    def sent(i):
        by = SENDS[i]
        return pltpu.make_async_remote_copy(
            src_ref=sources[i], dst_ref=targets[i], send_sem=send_sem.at[i], recv_sem=recv_sem.at[i],
            device_id=(fg + by[0], sp + by[1]), device_id_type=MESH,
        )

    above, below = sp > 0, sp < last_sp
    sends = [there(by) for by in SENDS[:4]] + [(fg < last_fg) & side for side in (above, below)] * 2
    arrives = [there(by, True) for by in SENDS[:4]] + [(fg > 0) & side for side in (above, below)] * 2

    def start(*which):
        for i in which:
            @pl.when(sends[i])
            def _():
                sent(i).start()

    def arrived(*which):
        for i in which:
            @pl.when(arrives[i])
            def _():
                sent(i).wait_recv()

    start(0, 1, 2, 3)

    @pl.when(fg == 0)
    def _():
        x[0:2] = jnp.zeros((2, rows, cols, width), BF16)
        halo[:, 0:2] = jnp.zeros((2, 2, cols, width), BF16)

    for side, there_is in enumerate((above, below)):
        @pl.when(jnp.logical_not(there_is))
        def _():
            halo[side] = jnp.zeros((frames + 2, cols, width), BF16)

    for load in loads[1:]:
        load.wait()

    def inner(n, carry):
        l = frames - 1 - n
        for j in range(4):
            i = 4 * l + j - 4
            for t in range(0, rows, 2):
                a = jnp.concatenate([x[l + k, t:t + 2].reshape(2 * cols, width) for k in range(3)], axis=1)
                up[i, t * cols:(t + 2) * cols, :] = activation(a, j, tw, tb)
            for p in range(rows // 2 - 1):
                row = lambda q: up[i, pl.ds((2 * p + q) * cols, cols), :]
                for h, value in enumerate(row_pair(row, cols, w01, w2, left, mid, right, sb, p)):
                    out_ref[i, 2 * p + 1 + h] = value
        return carry

    def rim(n, carry):
        l = frames - 1 - n
        for j in range(4):
            i = 4 * l + j - 4
            a = jnp.concatenate([halo[:, l + k].reshape(2 * cols, width) for k in range(3)], axis=1)
            act = activation(a, j, tw, tb)
            zero = jnp.zeros((cols, width), BF16)
            row = lambda h: up[i, pl.ds(h * cols, cols), :]
            first = [jnp.where(above, act[:cols], zero), row(0), row(1)]
            final = [row(rows - 2), row(rows - 1), jnp.where(below, act[cols:], zero)]
            a = jnp.concatenate([jnp.concatenate(first, axis=1), jnp.concatenate(final, axis=1)], axis=0)
            r = jnp.dot(a, w3[...], preferred_element_type=F32)
            for h in range(2):
                part = r[h * cols:(h + 1) * cols]
                left[h, 8:8 + cols, :] = part[:, :wide]
                right[h, 0:cols, :] = part[:, 2 * wide:]
                total = left[h, 7:7 + cols, :] + (part[:, wide:2 * wide] + sb[...]) + right[h, 1:1 + cols, :]
                out_ref[i, h * (rows - 1)] = total.astype(BF16)
        return carry

    lax.fori_loop(0, frames - 2, inner, 0)
    arrived(2)
    inner(frames - 2, 0)
    arrived(0, 1)
    start(4, 5, 6, 7)
    lax.fori_loop(0, frames - 2, rim, 0)
    arrived(4, 5)
    rim(frames - 2, 0)
    arrived(3, 6, 7)

    for i in range(len(SENDS)):
        @pl.when(sends[i])
        def _():
            sent(i).wait_send()


def frames_call(sizes, latent, tw, tb, sw, sb):
    frames, rows, cols, width = latent.shape
    wide = sw.shape[3]
    vmem = pl.BlockSpec(memory_space=pltpu.VMEM)
    hbm = pl.BlockSpec(memory_space=pl.ANY)
    out_shape = [
        pltpu.VMEM((4 * frames - 3, rows, cols, wide), BF16),
        pltpu.VMEM((frames + 2, rows, cols, width), BF16),
        pltpu.VMEM((2, frames + 2, cols, width), BF16),
        pltpu.VMEM(tw.shape, BF16),
        pltpu.VMEM(tb.shape, F32),
        pltpu.VMEM(sb.shape, F32),
        pltpu.VMEM((3 * width, 2 * wide), BF16),
        pltpu.VMEM((4 * width, 2 * wide), BF16),
    ]
    return pl.pallas_call(
        functools.partial(frames_kernel, sizes),
        in_specs=[hbm] * 5,
        out_specs=[vmem] * len(out_shape),
        out_shape=out_shape,
        scratch_shapes=[
            pltpu.VMEM((4 * frames - 4, rows * cols, width), BF16),
            pltpu.VMEM(sw.shape, BF16),
            pltpu.VMEM((3 * width, 3 * wide), BF16),
            pltpu.VMEM((rows, cols + 8, wide), F32),
            pltpu.VMEM((rows, cols, wide), F32),
            pltpu.VMEM((rows, cols + 8, wide), F32),
            pltpu.SemaphoreType.DMA((frames + 4,)),
            pltpu.SemaphoreType.DMA((len(SENDS),)),
            pltpu.SemaphoreType.DMA((len(SENDS),)),
        ],
        compiler_params=pltpu.CompilerParams(
            collective_id=0, has_side_effects=True, vmem_limit_bytes=LIMIT
        ),
        cost_estimate=pl.CostEstimate(flops=28 * 10**9, bytes_accessed=16 * 10**6, transcendentals=10**7),
        name="frames",
    )(latent, tw, tb, sw, sb)


def finish_kernel(counts_ref, late_ref, x, halo, tw, tb, sb, w01, w2, out_ref,
                  early, up, left, mid, right, sem):
    rows, cols, width = x.shape[1:]
    fg, sp = lax.axis_index("fg"), lax.axis_index("sp")
    last_sp = lax.axis_size("sp") - 1
    limit = counts_ref[fg]

    def copy(source, f):
        return pltpu.make_async_copy(source, out_ref.at[f], sem.at[f])

    late = late_ref.shape[0] - 1
    for f in range(late):
        copy(late_ref.at[jnp.where(4 + f < limit, f, late)], 4 + f).start()
    early[4] = jnp.zeros(early.shape[1:], BF16)
    zero_rims(left, right, cols)

    def rows_of(t, k):
        if t == 0:
            return jnp.concatenate([halo[0, k], x[k, 0]], axis=0)
        if t == rows:
            return jnp.concatenate([x[k, rows - 1], halo[1, k]], axis=0)
        return x[k, t - 1:t + 1].reshape(2 * cols, width)

    for j in range(4):
        for t in range(0, rows + 2, 2):
            a = jnp.concatenate([rows_of(t, k) for k in range(3)], axis=1)
            act = activation(a, j, tw, tb)
            none = jnp.zeros((cols, width), BF16)
            first = jnp.where(sp > 0, act[:cols], none) if t == 0 else act[:cols]
            second = jnp.where(sp < last_sp, act[cols:], none) if t == rows else act[cols:]
            up[j, t * cols:(t + 1) * cols, :] = first
            up[j, (t + 1) * cols:(t + 2) * cols, :] = second

        for p in range(rows // 2):
            row = lambda q: up[j, pl.ds((2 * p + q) * cols, cols), :]
            for h, value in enumerate(row_pair(row, cols, w01, w2, left, mid, right, sb, p)):
                early[j, 2 * p + h] = value
        copy(early.at[jnp.where(j < limit, j, 4)], j).start()

    for f in range(late + 4):
        copy(early.at[4], f).wait()


def finish_call(counts, late, x, *args):
    _, rows, cols, wide = late.shape
    width = x.shape[3]
    shape = (late.shape[0] + 3, rows, cols, wide)
    vmem = pl.BlockSpec(memory_space=pltpu.VMEM)
    return pl.pallas_call(
        finish_kernel,
        in_specs=[pl.BlockSpec(memory_space=pltpu.SMEM)] + [vmem] * (2 + len(args)),
        out_specs=pl.BlockSpec(memory_space=pl.ANY),
        out_shape=jax.ShapeDtypeStruct(shape, BF16),
        scratch_shapes=[
            pltpu.VMEM((5,) + shape[1:], BF16),
            pltpu.VMEM((4, (rows + 2) * cols, width), BF16),
            pltpu.VMEM((rows, cols + 8, wide), F32),
            pltpu.VMEM((rows, cols, wide), F32),
            pltpu.VMEM((rows, cols + 8, wide), F32),
            pltpu.SemaphoreType.DMA((shape[0],)),
        ],
        compiler_params=pltpu.CompilerParams(vmem_limit_bytes=24 * 1024 * 1024),
        cost_estimate=pl.CostEstimate(flops=9 * 10**9, bytes_accessed=16 * 10**6, transcendentals=10**6),
        name="finish",
    )(counts, late, x, *args)


def on_device(sizes, latent, temporal_weight, temporal_bias, spatial_weight, spatial_bias, counts):
    width = latent.shape[3]
    tw = temporal_weight.reshape(3 * width, 4 * width)
    args = (tw, temporal_bias.reshape(1, -1), spatial_weight, spatial_bias.reshape(1, -1))
    return finish_call(counts, *frames_call(sizes, latent, *args))


def solution(mesh):
    sizes = (mesh.shape["fg"], mesh.shape["sp"])
    return jax.shard_map(
        functools.partial(on_device, sizes),
        mesh=mesh,
        in_specs=(P("fg", "sp", None, None), P(), P(), P(), P(), P()),
        out_specs=P("fg", "sp", None, None),
        check_vma=False,
    )
```

```python
import functools

import jax
import jax.numpy as jnp
from jax import lax
from jax.experimental import pallas as pl
from jax.experimental.pallas import tpu as pltpu
from jax.sharding import PartitionSpec as P

F32, BF16 = jnp.float32, jnp.bfloat16
LIMIT = 40 * 1024 * 1024
MESH = pl.DeviceIdType.MESH
SENDS = ((0, 1), (0, -1)) + ((1, 0),) * 6
NEIGHBOURS = ((0, 1), (0, -1), (1, 0), (-1, 0))


def silu(pre):
    half = pre
    return half + half * jnp.tanh(half)


def fill_weights(sw_ref, w01, w2):
    depth, wide = sw_ref.shape[2], sw_ref.shape[3]
    zero = jnp.zeros((depth, wide), BF16)
    for dy in range(3):
        at = pl.ds(dy * depth, depth)
        w01[at, :wide] = sw_ref[dy, 0]
        w01[at, wide:] = sw_ref[dy, 1]
    for q in range(4):
        at = pl.ds(q * depth, depth)
        w2[at, :wide] = sw_ref[q, 2] if q < 3 else zero
        w2[at, wide:] = sw_ref[q - 1, 2] if q > 0 else zero


def activation(a, j, tw_ref, tb_ref):
    width = tw_ref.shape[1] // 4
    columns = pl.ds(pl.multiple_of(j * width, width), width)
    pre = jnp.dot(a, tw_ref[:, columns], preferred_element_type=F32) + tb_ref[:, columns]
    return silu(pre).astype(BF16)


def zero_rims(left, right, cols):
    n, _, wide = left.shape
    left[:, 0:8, :] = jnp.zeros((n, 8, wide), F32)
    right[:, cols:cols + 8, :] = jnp.zeros((n, 8, wide), F32)


def row_pair(row, cols, w01, w2, left, mid, right, sb_ref, p):
    wide = sb_ref.shape[1]
    taps = [row(q) for q in range(4)]
    a = jnp.concatenate([jnp.concatenate(taps[h:h + 3], axis=1) for h in range(2)], axis=0)
    r = jnp.dot(a, w01[...], preferred_element_type=F32)
    s = jnp.dot(jnp.concatenate(taps, axis=1), w2[...], preferred_element_type=F32)
    rows = []
    for h in range(2):
        left[2 * p + h, 8:8 + cols, :] = r[h * cols:(h + 1) * cols, :wide]
        right[2 * p + h, 0:cols, :] = s[:, h * wide:(h + 1) * wide]
        mid[2 * p + h] = r[h * cols:(h + 1) * cols, wide:]
        total = left[2 * p + h, 7:7 + cols, :] + mid[2 * p + h] + right[2 * p + h, 1:1 + cols, :] + sb_ref[...]
        rows.append(total.astype(BF16))
    return rows


def frames_kernel(sizes, latent_ref, tw_ref, tb_ref, sw_ref, sb_ref,
                  out_ref, x, halo, tw, tb, sb, w01, w2,
                  up, edge, sw, w3, left, mid, right, load_sem, send_sem, recv_sem):
    frames, rows, cols, width = latent_ref.shape
    wide = sb_ref.shape[1]
    fg, sp = lax.axis_index("fg"), lax.axis_index("sp")
    last_fg, last_sp = sizes[0] - 1, sizes[1] - 1

    def there(by, back=False):
        f, s = (fg - by[0], sp - by[1]) if back else (fg + by[0], sp + by[1])
        return (f >= 0) & (f <= last_fg) & (s >= 0) & (s <= last_sp)

    barrier = pltpu.get_barrier_semaphore()
    for by in NEIGHBOURS:
        @pl.when(there(by))
        def _():
            pl.semaphore_signal(barrier, inc=1, device_id=(fg + by[0], sp + by[1]), device_id_type=MESH)

    moves = [(sw_ref, sw), (tw_ref, tw), (tb_ref, tb), (sb_ref, sb)]
    moves += [(latent_ref.at[f], x.at[2 + f]) for f in range(frames)]
    loads = [pltpu.make_async_copy(source, target, load_sem.at[n]) for n, (source, target) in enumerate(moves)]
    for load in loads:
        load.start()

    out_ref[4 * frames - 4] = jnp.zeros(out_ref.shape[1:], BF16)
    zero_rims(left, right, cols)
    loads[0].wait()
    fill_weights(sw, w01, w2)
    for dy in range(3):
        for dx in range(3):
            w3[dy * width:(dy + 1) * width, dx * wide:(dx + 1) * wide] = sw[dy, dx]

    near = [(at > 0).astype(jnp.int32) + (at < n).astype(jnp.int32) for at, n in ((fg, last_fg), (sp, last_sp))]
    pl.semaphore_wait(barrier, near[0] + near[1])

    own = pl.ds(2, frames)
    sources = [latent_ref.at[:, rows - 1], latent_ref.at[:, 0], latent_ref.at[frames - 1], latent_ref.at[frames - 2]]
    targets = [halo.at[0, own], halo.at[1, own], x.at[1], x.at[0]]
    for k in (1, 0):
        sources += [halo.at[side, frames + k] for side in range(2)]
        targets += [halo.at[side, k] for side in range(2)]

    def sent(i):
        by = SENDS[i]
        return pltpu.make_async_remote_copy(
            src_ref=sources[i], dst_ref=targets[i], send_sem=send_sem.at[i], recv_sem=recv_sem.at[i],
            device_id=(fg + by[0], sp + by[1]), device_id_type=MESH,
        )

    above, below = sp > 0, sp < last_sp
    sends = [there(by) for by in SENDS[:4]] + [(fg < last_fg) & side for side in (above, below)] * 2
    arrives = [there(by, True) for by in SENDS[:4]] + [(fg > 0) & side for side in (above, below)] * 2

    def start(*which):
        for i in which:
            @pl.when(sends[i])
            def _():
                sent(i).start()

    def arrived(*which):
        for i in which:
            @pl.when(arrives[i])
            def _():
                sent(i).wait_recv()

    start(0, 1, 2, 3)

    @pl.when(fg == 0)
    def _():
        x[0:2] = jnp.zeros((2, rows, cols, width), BF16)
        halo[:, 0:2] = jnp.zeros((2, 2, cols, width), BF16)

    for side, there_is in enumerate((above, below)):
        @pl.when(jnp.logical_not(there_is))
        def _():
            halo[side] = jnp.zeros((frames + 2, cols, width), BF16)

    for load in loads[1:]:
        load.wait()
    tw[...] = tw[...] * 0.5
    tb[...] = tb[...] * 0.5

    def inner(n, carry):
        l = frames - 1 - n
        for j in range(4):
            i = 4 * l + j - 4
            for t in range(0, rows, 2):
                a = jnp.concatenate([x[l + k, t:t + 2].reshape(2 * cols, width) for k in range(3)], axis=1)
                up[i, t * cols:(t + 2) * cols, :] = activation(a, j, tw, tb)
            for p in range(rows // 2 - 1):
                row = lambda q: up[i, pl.ds((2 * p + q) * cols, cols), :]
                for h, value in enumerate(row_pair(row, cols, w01, w2, left, mid, right, sb, p)):
                    out_ref[i, 2 * p + 1 + h] = value
        return carry

    def rim(n, carry):
        l = frames - 1 - n

        def temporal(j):
            a = jnp.concatenate([halo[:, l + k].reshape(2 * cols, width) for k in range(3)], axis=1)
            act = activation(a, j, tw, tb)
            zero = jnp.zeros((cols, width), BF16)
            edge[j][:cols] = jnp.where(above, act[:cols], zero)
            edge[j][cols:] = jnp.where(below, act[cols:], zero)

        def spatial(j):
            i = 4 * l + j - 4
            row = lambda h: up[i, pl.ds(h * cols, cols), :]
            first = [edge[j][:cols], row(0), row(1)]
            final = [row(rows - 2), row(rows - 1), edge[j][cols:]]
            a = jnp.concatenate([jnp.concatenate(first, axis=1), jnp.concatenate(final, axis=1)], axis=0)
            r = jnp.dot(a, w3[...], preferred_element_type=F32)
            for h in range(2):
                part = r[h * cols:(h + 1) * cols]
                left[2 * j + h, 8:8 + cols, :] = part[:, :wide]
                right[2 * j + h, 0:cols, :] = part[:, 2 * wide:]
                here = part[:, wide:2 * wide] + sb[...]
                total = left[2 * j + h, 7:7 + cols, :] + here + right[2 * j + h, 1:1 + cols, :]
                out_ref[i, h * (rows - 1)] = total.astype(BF16)

        temporal(0)
        temporal(1)
        spatial(0)
        temporal(2)
        spatial(1)
        temporal(3)
        spatial(2)
        spatial(3)
        return carry

    lax.fori_loop(0, frames - 2, inner, 0)
    arrived(2)
    inner(frames - 2, 0)
    arrived(0, 1)
    start(4, 5, 6, 7)
    lax.fori_loop(0, frames - 2, rim, 0)
    arrived(4, 5)
    rim(frames - 2, 0)
    arrived(3, 6, 7)

    for i in range(len(SENDS)):
        @pl.when(sends[i])
        def _():
            sent(i).wait_send()


def frames_call(sizes, latent, tw, tb, sw, sb):
    frames, rows, cols, width = latent.shape
    wide = sw.shape[3]
    vmem = pl.BlockSpec(memory_space=pltpu.VMEM)
    hbm = pl.BlockSpec(memory_space=pl.ANY)
    out_shape = [
        pltpu.VMEM((4 * frames - 3, rows, cols, wide), BF16),
        pltpu.VMEM((frames + 2, rows, cols, width), BF16),
        pltpu.VMEM((2, frames + 2, cols, width), BF16),
        pltpu.VMEM(tw.shape, BF16),
        pltpu.VMEM(tb.shape, F32),
        pltpu.VMEM(sb.shape, F32),
        pltpu.VMEM((3 * width, 2 * wide), BF16),
        pltpu.VMEM((4 * width, 2 * wide), BF16),
    ]
    return pl.pallas_call(
        functools.partial(frames_kernel, sizes),
        in_specs=[hbm] * 5,
        out_specs=[vmem] * len(out_shape),
        out_shape=out_shape,
        scratch_shapes=[
            pltpu.VMEM((4 * frames - 4, rows * cols, width), BF16),
            [pltpu.VMEM((2 * cols, width), BF16)] * 4,
            pltpu.VMEM(sw.shape, BF16),
            pltpu.VMEM((3 * width, 3 * wide), BF16),
            pltpu.VMEM((rows, cols + 8, wide), F32),
            pltpu.VMEM((rows, cols, wide), F32),
            pltpu.VMEM((rows, cols + 8, wide), F32),
            pltpu.SemaphoreType.DMA((frames + 4,)),
            pltpu.SemaphoreType.DMA((len(SENDS),)),
            pltpu.SemaphoreType.DMA((len(SENDS),)),
        ],
        compiler_params=pltpu.CompilerParams(
            collective_id=0, has_side_effects=True, vmem_limit_bytes=LIMIT
        ),
        cost_estimate=pl.CostEstimate(flops=28 * 10**9, bytes_accessed=16 * 10**6, transcendentals=10**7),
        name="frames",
    )(latent, tw, tb, sw, sb)


def finish_kernel(counts_ref, late_ref, x, halo, tw, tb, sb, w01, w2, out_ref,
                  early, up, left, mid, right, sem):
    rows, cols, width = x.shape[1:]
    fg, sp = lax.axis_index("fg"), lax.axis_index("sp")
    last_sp = lax.axis_size("sp") - 1
    limit = counts_ref[fg]

    def copy(source, f):
        return pltpu.make_async_copy(source, out_ref.at[f], sem.at[f])

    late = late_ref.shape[0] - 1
    for f in range(late):
        copy(late_ref.at[jnp.where(4 + f < limit, f, late)], 4 + f).start()
    early[4] = jnp.zeros(early.shape[1:], BF16)
    zero_rims(left, right, cols)

    def rows_of(t, k):
        if t == 0:
            return jnp.concatenate([halo[0, k], x[k, 0]], axis=0)
        if t == rows:
            return jnp.concatenate([x[k, rows - 1], halo[1, k]], axis=0)
        return x[k, t - 1:t + 1].reshape(2 * cols, width)

    for j in range(4):
        for t in range(0, rows + 2, 2):
            a = jnp.concatenate([rows_of(t, k) for k in range(3)], axis=1)
            act = activation(a, j, tw, tb)
            none = jnp.zeros((cols, width), BF16)
            first = jnp.where(sp > 0, act[:cols], none) if t == 0 else act[:cols]
            second = jnp.where(sp < last_sp, act[cols:], none) if t == rows else act[cols:]
            up[j, t * cols:(t + 1) * cols, :] = first
            up[j, (t + 1) * cols:(t + 2) * cols, :] = second

        for p in range(rows // 2):
            row = lambda q: up[j, pl.ds((2 * p + q) * cols, cols), :]
            for h, value in enumerate(row_pair(row, cols, w01, w2, left, mid, right, sb, p)):
                early[j, 2 * p + h] = value
        copy(early.at[jnp.where(j < limit, j, 4)], j).start()

    for f in range(late + 4):
        copy(early.at[4], f).wait()


def finish_call(counts, late, x, *args):
    _, rows, cols, wide = late.shape
    width = x.shape[3]
    shape = (late.shape[0] + 3, rows, cols, wide)
    vmem = pl.BlockSpec(memory_space=pltpu.VMEM)
    return pl.pallas_call(
        finish_kernel,
        in_specs=[pl.BlockSpec(memory_space=pltpu.SMEM)] + [vmem] * (2 + len(args)),
        out_specs=pl.BlockSpec(memory_space=pl.ANY),
        out_shape=jax.ShapeDtypeStruct(shape, BF16),
        scratch_shapes=[
            pltpu.VMEM((5,) + shape[1:], BF16),
            pltpu.VMEM((4, (rows + 2) * cols, width), BF16),
            pltpu.VMEM((rows, cols + 8, wide), F32),
            pltpu.VMEM((rows, cols, wide), F32),
            pltpu.VMEM((rows, cols + 8, wide), F32),
            pltpu.SemaphoreType.DMA((shape[0],)),
        ],
        compiler_params=pltpu.CompilerParams(vmem_limit_bytes=24 * 1024 * 1024),
        cost_estimate=pl.CostEstimate(flops=9 * 10**9, bytes_accessed=16 * 10**6, transcendentals=10**6),
        name="finish",
    )(counts, late, x, *args)


def on_device(sizes, latent, temporal_weight, temporal_bias, spatial_weight, spatial_bias, counts):
    width = latent.shape[3]
    tw = temporal_weight.reshape(3 * width, 4 * width)
    args = (tw, temporal_bias.reshape(1, -1), spatial_weight, spatial_bias.reshape(1, -1))
    return finish_call(counts, *frames_call(sizes, latent, *args))


def solution(mesh):
    sizes = (mesh.shape["fg"], mesh.shape["sp"])
    return jax.shard_map(
        functools.partial(on_device, sizes),
        mesh=mesh,
        in_specs=(P("fg", "sp", None, None), P(), P(), P(), P(), P()),
        out_specs=P("fg", "sp", None, None),
        check_vma=False,
    )
```

```python
import functools

import jax
import jax.numpy as jnp
from jax import lax
from jax.experimental import pallas as pl
from jax.experimental.pallas import tpu as pltpu
from jax.sharding import PartitionSpec as P

F32, BF16 = jnp.float32, jnp.bfloat16
LIMIT = 40 * 1024 * 1024
MESH = pl.DeviceIdType.MESH
SENDS = ((0, 1), (0, -1)) + ((1, 0),) * 6
NEIGHBOURS = ((0, 1), (0, -1), (1, 0), (-1, 0))


def silu(pre):
    half = pre
    return half + half * jnp.tanh(half)


def fill_weights(sw_ref, w01, w2):
    depth, wide = sw_ref.shape[2], sw_ref.shape[3]
    zero = jnp.zeros((depth, wide), BF16)
    for dy in range(3):
        at = pl.ds(dy * depth, depth)
        w01[at, :wide] = sw_ref[dy, 0]
        w01[at, wide:] = sw_ref[dy, 1]
    for q in range(4):
        at = pl.ds(q * depth, depth)
        w2[at, :wide] = sw_ref[q, 2] if q < 3 else zero
        w2[at, wide:] = sw_ref[q - 1, 2] if q > 0 else zero


def activation(a, j, tw_ref, tb_ref):
    width = tw_ref.shape[1] // 4
    columns = pl.ds(pl.multiple_of(j * width, width), width)
    pre = jnp.dot(a, tw_ref[:, columns], preferred_element_type=F32) + tb_ref[:, columns]
    return silu(pre).astype(BF16)


def zero_rims(left, right, cols):
    n, _, wide = left.shape
    left[:, 0:8, :] = jnp.zeros((n, 8, wide), F32)
    right[:, cols:cols + 8, :] = jnp.zeros((n, 8, wide), F32)


def row_pair(row, cols, w01, w2, left, mid, right, sb_ref, p):
    wide = sb_ref.shape[1]
    taps = [row(q) for q in range(4)]
    a = jnp.concatenate([jnp.concatenate(taps[h:h + 3], axis=1) for h in range(2)], axis=0)
    r = jnp.dot(a, w01[...], preferred_element_type=F32)
    s = jnp.dot(jnp.concatenate(taps, axis=1), w2[...], preferred_element_type=F32)
    rows = []
    for h in range(2):
        left[2 * p + h, 8:8 + cols, :] = r[h * cols:(h + 1) * cols, :wide]
        right[2 * p + h, 0:cols, :] = s[:, h * wide:(h + 1) * wide]
        mid[2 * p + h] = r[h * cols:(h + 1) * cols, wide:]
        total = pltpu.roll(left[2 * p + h], 1, 0)[8:] + mid[2 * p + h] + pltpu.roll(right[2 * p + h], cols + 7, 0)[:cols] + sb_ref[...]
        rows.append(total.astype(BF16))
    return rows


def frames_kernel(sizes, latent_ref, tw_ref, tb_ref, sw_ref, sb_ref,
                  out_ref, x, halo, tw, tb, sb, w01, w2,
                  up, edge, sw, w3, left, mid, right, load_sem, send_sem, recv_sem):
    frames, rows, cols, width = latent_ref.shape
    wide = sb_ref.shape[1]
    fg, sp = lax.axis_index("fg"), lax.axis_index("sp")
    last_fg, last_sp = sizes[0] - 1, sizes[1] - 1

    def there(by, back=False):
        f, s = (fg - by[0], sp - by[1]) if back else (fg + by[0], sp + by[1])
        return (f >= 0) & (f <= last_fg) & (s >= 0) & (s <= last_sp)

    barrier = pltpu.get_barrier_semaphore()
    for by in NEIGHBOURS:
        @pl.when(there(by))
        def _():
            pl.semaphore_signal(barrier, inc=1, device_id=(fg + by[0], sp + by[1]), device_id_type=MESH)

    moves = [(sw_ref, sw), (tw_ref, tw), (tb_ref, tb), (sb_ref, sb)]
    moves += [(latent_ref.at[f], x.at[2 + f]) for f in range(frames)]
    loads = [pltpu.make_async_copy(source, target, load_sem.at[n]) for n, (source, target) in enumerate(moves)]
    for load in loads:
        load.start()

    out_ref[4 * frames - 4] = jnp.zeros(out_ref.shape[1:], BF16)
    zero_rims(left, right, cols)
    loads[0].wait()
    fill_weights(sw, w01, w2)
    for dy in range(3):
        for dx in range(3):
            w3[dy * width:(dy + 1) * width, dx * wide:(dx + 1) * wide] = sw[dy, dx]

    near = [(at > 0).astype(jnp.int32) + (at < n).astype(jnp.int32) for at, n in ((fg, last_fg), (sp, last_sp))]
    pl.semaphore_wait(barrier, near[0] + near[1])

    own = pl.ds(2, frames)
    sources = [latent_ref.at[:, rows - 1], latent_ref.at[:, 0], latent_ref.at[frames - 1], latent_ref.at[frames - 2]]
    targets = [halo.at[0, own], halo.at[1, own], x.at[1], x.at[0]]
    for k in (1, 0):
        sources += [halo.at[side, frames + k] for side in range(2)]
        targets += [halo.at[side, k] for side in range(2)]

    def sent(i):
        by = SENDS[i]
        return pltpu.make_async_remote_copy(
            src_ref=sources[i], dst_ref=targets[i], send_sem=send_sem.at[i], recv_sem=recv_sem.at[i],
            device_id=(fg + by[0], sp + by[1]), device_id_type=MESH,
        )

    above, below = sp > 0, sp < last_sp
    sends = [there(by) for by in SENDS[:4]] + [(fg < last_fg) & side for side in (above, below)] * 2
    arrives = [there(by, True) for by in SENDS[:4]] + [(fg > 0) & side for side in (above, below)] * 2

    def start(*which):
        for i in which:
            @pl.when(sends[i])
            def _():
                sent(i).start()

    def arrived(*which):
        for i in which:
            @pl.when(arrives[i])
            def _():
                sent(i).wait_recv()

    start(0, 1, 2, 3)

    @pl.when(fg == 0)
    def _():
        x[0:2] = jnp.zeros((2, rows, cols, width), BF16)
        halo[:, 0:2] = jnp.zeros((2, 2, cols, width), BF16)

    for side, there_is in enumerate((above, below)):
        @pl.when(jnp.logical_not(there_is))
        def _():
            halo[side] = jnp.zeros((frames + 2, cols, width), BF16)

    for load in loads[1:]:
        load.wait()
    tw[...] = tw[...] * 0.5
    tb[...] = tb[...] * 0.5

    def inner(n, carry):
        l = frames - 1 - n
        for j in range(4):
            i = 4 * l + j - 4
            for t in range(0, rows, 2):
                a = jnp.concatenate([x[l + k, t:t + 2].reshape(2 * cols, width) for k in range(3)], axis=1)
                up[i, t * cols:(t + 2) * cols, :] = activation(a, j, tw, tb)
            for p in range(rows // 2 - 1):
                row = lambda q: up[i, pl.ds((2 * p + q) * cols, cols), :]
                for h, value in enumerate(row_pair(row, cols, w01, w2, left, mid, right, sb, p)):
                    out_ref[i, 2 * p + 1 + h] = value
        return carry

    def rim(n, carry):
        l = frames - 1 - n

        def temporal(j):
            a = jnp.concatenate([halo[:, l + k].reshape(2 * cols, width) for k in range(3)], axis=1)
            act = activation(a, j, tw, tb)
            zero = jnp.zeros((cols, width), BF16)
            edge[j][:cols] = jnp.where(above, act[:cols], zero)
            edge[j][cols:] = jnp.where(below, act[cols:], zero)

        def spatial(j):
            i = 4 * l + j - 4
            row = lambda h: up[i, pl.ds(h * cols, cols), :]
            first = [edge[j][:cols], row(0), row(1)]
            final = [row(rows - 2), row(rows - 1), edge[j][cols:]]
            a = jnp.concatenate([jnp.concatenate(first, axis=1), jnp.concatenate(final, axis=1)], axis=0)
            r = jnp.dot(a, w3[...], preferred_element_type=F32)
            for h in range(2):
                part = r[h * cols:(h + 1) * cols]
                left[2 * j + h, 8:8 + cols, :] = part[:, :wide]
                right[2 * j + h, 0:cols, :] = part[:, 2 * wide:]
                here = part[:, wide:2 * wide] + sb[...]
                total = pltpu.roll(left[2 * j + h], 1, 0)[8:] + here + pltpu.roll(right[2 * j + h], cols + 7, 0)[:cols]
                out_ref[i, h * (rows - 1)] = total.astype(BF16)

        temporal(0)
        temporal(1)
        spatial(0)
        temporal(2)
        spatial(1)
        temporal(3)
        spatial(2)
        spatial(3)
        return carry

    lax.fori_loop(0, frames - 2, inner, 0)
    arrived(2)
    inner(frames - 2, 0)
    arrived(0, 1)
    start(4, 5, 6, 7)
    lax.fori_loop(0, frames - 2, rim, 0)
    arrived(4, 5)
    rim(frames - 2, 0)
    arrived(3, 6, 7)

    for i in range(len(SENDS)):
        @pl.when(sends[i])
        def _():
            sent(i).wait_send()


def frames_call(sizes, latent, tw, tb, sw, sb):
    frames, rows, cols, width = latent.shape
    wide = sw.shape[3]
    vmem = pl.BlockSpec(memory_space=pltpu.VMEM)
    hbm = pl.BlockSpec(memory_space=pl.ANY)
    out_shape = [
        pltpu.VMEM((4 * frames - 3, rows, cols, wide), BF16),
        pltpu.VMEM((frames + 2, rows, cols, width), BF16),
        pltpu.VMEM((2, frames + 2, cols, width), BF16),
        pltpu.VMEM(tw.shape, BF16),
        pltpu.VMEM(tb.shape, F32),
        pltpu.VMEM(sb.shape, F32),
        pltpu.VMEM((3 * width, 2 * wide), BF16),
        pltpu.VMEM((4 * width, 2 * wide), BF16),
    ]
    return pl.pallas_call(
        functools.partial(frames_kernel, sizes),
        in_specs=[hbm] * 5,
        out_specs=[vmem] * len(out_shape),
        out_shape=out_shape,
        scratch_shapes=[
            pltpu.VMEM((4 * frames - 4, rows * cols, width), BF16),
            [pltpu.VMEM((2 * cols, width), BF16)] * 4,
            pltpu.VMEM(sw.shape, BF16),
            pltpu.VMEM((3 * width, 3 * wide), BF16),
            pltpu.VMEM((rows, cols + 8, wide), F32),
            pltpu.VMEM((rows, cols, wide), F32),
            pltpu.VMEM((rows, cols + 8, wide), F32),
            pltpu.SemaphoreType.DMA((frames + 4,)),
            pltpu.SemaphoreType.DMA((len(SENDS),)),
            pltpu.SemaphoreType.DMA((len(SENDS),)),
        ],
        compiler_params=pltpu.CompilerParams(
            collective_id=0, has_side_effects=True, vmem_limit_bytes=LIMIT
        ),
        cost_estimate=pl.CostEstimate(flops=28 * 10**9, bytes_accessed=16 * 10**6, transcendentals=10**7),
        name="frames",
    )(latent, tw, tb, sw, sb)


def finish_kernel(counts_ref, late_ref, x, halo, tw, tb, sb, w01, w2, out_ref,
                  early, up, left, mid, right, sem):
    rows, cols, width = x.shape[1:]
    fg, sp = lax.axis_index("fg"), lax.axis_index("sp")
    last_sp = lax.axis_size("sp") - 1
    limit = counts_ref[fg]

    def copy(source, f):
        return pltpu.make_async_copy(source, out_ref.at[f], sem)

    late = late_ref.shape[0] - 1
    for f in range(late):
        copy(late_ref.at[jnp.where(4 + f < limit, f, late)], 4 + f).start()
    early[4] = jnp.zeros(early.shape[1:], BF16)
    zero_rims(left, right, cols)

    def rows_of(t, k):
        if t == 0:
            return jnp.concatenate([halo[0, k], x[k, 0]], axis=0)
        if t == rows:
            return jnp.concatenate([x[k, rows - 1], halo[1, k]], axis=0)
        return x[k, t - 1:t + 1].reshape(2 * cols, width)

    for j in range(4):
        for t in range(0, rows + 2, 2):
            a = jnp.concatenate([rows_of(t, k) for k in range(3)], axis=1)
            act = activation(a, j, tw, tb)
            none = jnp.zeros((cols, width), BF16)
            first = jnp.where(sp > 0, act[:cols], none) if t == 0 else act[:cols]
            second = jnp.where(sp < last_sp, act[cols:], none) if t == rows else act[cols:]
            up[j, t * cols:(t + 1) * cols, :] = first
            up[j, (t + 1) * cols:(t + 2) * cols, :] = second

        for p in range(rows // 2):
            row = lambda q: up[j, pl.ds((2 * p + q) * cols, cols), :]
            for h, value in enumerate(row_pair(row, cols, w01, w2, left, mid, right, sb, p)):
                early[j, 2 * p + h] = value
        copy(early.at[jnp.where(j < limit, j, 4)], j).start()

    pltpu.make_async_copy(out_ref, out_ref, sem).wait()


def finish_call(counts, late, x, *args):
    _, rows, cols, wide = late.shape
    width = x.shape[3]
    shape = (late.shape[0] + 3, rows, cols, wide)
    vmem = pl.BlockSpec(memory_space=pltpu.VMEM)
    return pl.pallas_call(
        finish_kernel,
        in_specs=[pl.BlockSpec(memory_space=pltpu.SMEM)] + [vmem] * (2 + len(args)),
        out_specs=pl.BlockSpec(memory_space=pl.ANY),
        out_shape=jax.ShapeDtypeStruct(shape, BF16),
        scratch_shapes=[
            pltpu.VMEM((5,) + shape[1:], BF16),
            pltpu.VMEM((4, (rows + 2) * cols, width), BF16),
            pltpu.VMEM((rows, cols + 8, wide), F32),
            pltpu.VMEM((rows, cols, wide), F32),
            pltpu.VMEM((rows, cols + 8, wide), F32),
            pltpu.SemaphoreType.DMA(()),
        ],
        compiler_params=pltpu.CompilerParams(vmem_limit_bytes=24 * 1024 * 1024),
        cost_estimate=pl.CostEstimate(flops=9 * 10**9, bytes_accessed=16 * 10**6, transcendentals=10**6),
        name="finish",
    )(counts, late, x, *args)


def on_device(sizes, latent, temporal_weight, temporal_bias, spatial_weight, spatial_bias, counts):
    width = latent.shape[3]
    tw = temporal_weight.reshape(3 * width, 4 * width)
    args = (tw, temporal_bias.reshape(1, -1), spatial_weight, spatial_bias.reshape(1, -1))
    return finish_call(counts, *frames_call(sizes, latent, *args))


def solution(mesh):
    sizes = (mesh.shape["fg"], mesh.shape["sp"])
    return jax.shard_map(
        functools.partial(on_device, sizes),
        mesh=mesh,
        in_specs=(P("fg", "sp", None, None), P(), P(), P(), P(), P()),
        out_specs=P("fg", "sp", None, None),
        check_vma=False,
    )
```

```python
import functools

import jax
import jax.numpy as jnp
from jax import lax
from jax.experimental import pallas as pl
from jax.experimental.pallas import tpu as pltpu
from jax.sharding import PartitionSpec as P

F32, BF16 = jnp.float32, jnp.bfloat16
LIMIT = 40 * 1024 * 1024
MESH = pl.DeviceIdType.MESH
SENDS = ((0, 1), (0, -1)) + ((1, 0),) * 6
NEIGHBOURS = ((0, 1), (0, -1), (1, 0), (-1, 0))


def silu(pre):
    half = pre
    return half + half * jnp.tanh(half)


def fill_weights(sw_ref, w01, w2):
    depth, wide = sw_ref.shape[2], sw_ref.shape[3]
    zero = jnp.zeros((depth, wide), BF16)
    for dy in range(3):
        at = pl.ds(dy * depth, depth)
        w01[at, :wide] = sw_ref[dy, 0]
        w01[at, wide:] = sw_ref[dy, 1]
    for q in range(4):
        at = pl.ds(q * depth, depth)
        w2[at, :wide] = sw_ref[q, 2] if q < 3 else zero
        w2[at, wide:] = sw_ref[q - 1, 2] if q > 0 else zero


def activation(a, j, tw_ref, tb_ref):
    width = tw_ref.shape[1] // 4
    columns = pl.ds(pl.multiple_of(j * width, width), width)
    pre = jnp.dot(a, tw_ref[:, columns], preferred_element_type=F32) + tb_ref[:, columns]
    return silu(pre).astype(BF16)


def zero_rims(left, right, cols):
    n, _, wide = left.shape
    left[:, 0:8, :] = jnp.zeros((n, 8, wide), F32)
    right[:, cols:cols + 8, :] = jnp.zeros((n, 8, wide), F32)


def row_pair(row, cols, w01, w2, left, mid, right, sb_ref, p):
    wide = sb_ref.shape[1]
    taps = [row(q) for q in range(4)]
    a = jnp.concatenate([jnp.concatenate(taps[h:h + 3], axis=1) for h in range(2)], axis=0)
    r = jnp.dot(a, w01[...], preferred_element_type=F32)
    s = jnp.dot(jnp.concatenate(taps, axis=1), w2[...], preferred_element_type=F32)
    rows = []
    for h in range(2):
        left[2 * p + h, 8:8 + cols, :] = r[h * cols:(h + 1) * cols, :wide]
        right[2 * p + h, 0:cols, :] = s[:, h * wide:(h + 1) * wide]
        here = r[h * cols:(h + 1) * cols, wide:] + sb_ref[...]
        total = pltpu.roll(left[2 * p + h], 1, 0)[8:] + here + pltpu.roll(right[2 * p + h], cols + 7, 0)[:cols]
        rows.append(total.astype(BF16))
    return rows


def frames_kernel(sizes, latent_ref, tw_ref, tb_ref, sw_ref, sb_ref,
                  out_ref, x, halo, tw, tb, sb, w01, w2,
                  up, edge, sw, w3, left, mid, right, load_sem, send_sem, recv_sem):
    frames, rows, cols, width = latent_ref.shape
    wide = sb_ref.shape[1]
    fg, sp = lax.axis_index("fg"), lax.axis_index("sp")
    last_fg, last_sp = sizes[0] - 1, sizes[1] - 1

    def there(by, back=False):
        f, s = (fg - by[0], sp - by[1]) if back else (fg + by[0], sp + by[1])
        return (f >= 0) & (f <= last_fg) & (s >= 0) & (s <= last_sp)

    barrier = pltpu.get_barrier_semaphore()
    for by in NEIGHBOURS:
        @pl.when(there(by))
        def _():
            pl.semaphore_signal(barrier, inc=1, device_id=(fg + by[0], sp + by[1]), device_id_type=MESH)

    moves = [(sw_ref, sw), (tw_ref, tw), (tb_ref, tb), (sb_ref, sb)]
    moves += [(latent_ref.at[f], x.at[2 + f]) for f in range(frames)]
    loads = [pltpu.make_async_copy(source, target, load_sem.at[n]) for n, (source, target) in enumerate(moves)]
    for load in loads:
        load.start()

    out_ref[4 * frames - 4] = jnp.zeros(out_ref.shape[1:], BF16)
    zero_rims(left, right, cols)
    loads[0].wait()
    fill_weights(sw, w01, w2)
    for dy in range(3):
        for dx in range(3):
            w3[dy * width:(dy + 1) * width, dx * wide:(dx + 1) * wide] = sw[dy, dx]

    for load in loads[1:4]:
        load.wait()
    tw[...] = tw[...] * 0.5
    tb[...] = tb[...] * 0.5

    near = [(at > 0).astype(jnp.int32) + (at < n).astype(jnp.int32) for at, n in ((fg, last_fg), (sp, last_sp))]
    pl.semaphore_wait(barrier, near[0] + near[1])

    own = pl.ds(2, frames)
    sources = [latent_ref.at[:, rows - 1], latent_ref.at[:, 0], latent_ref.at[frames - 1], latent_ref.at[frames - 2]]
    targets = [halo.at[0, own], halo.at[1, own], x.at[1], x.at[0]]
    for k in (1, 0):
        sources += [halo.at[side, frames + k] for side in range(2)]
        targets += [halo.at[side, k] for side in range(2)]

    def sent(i):
        by = SENDS[i]
        return pltpu.make_async_remote_copy(
            src_ref=sources[i], dst_ref=targets[i], send_sem=send_sem.at[i], recv_sem=recv_sem.at[i],
            device_id=(fg + by[0], sp + by[1]), device_id_type=MESH,
        )

    above, below = sp > 0, sp < last_sp
    sends = [there(by) for by in SENDS[:4]] + [(fg < last_fg) & side for side in (above, below)] * 2
    arrives = [there(by, True) for by in SENDS[:4]] + [(fg > 0) & side for side in (above, below)] * 2

    def start(*which):
        for i in which:
            @pl.when(sends[i])
            def _():
                sent(i).start()

    def arrived(*which):
        for i in which:
            @pl.when(arrives[i])
            def _():
                sent(i).wait_recv()

    start(0, 1, 2, 3)

    @pl.when(fg == 0)
    def _():
        x[0:2] = jnp.zeros((2, rows, cols, width), BF16)
        halo[:, 0:2] = jnp.zeros((2, 2, cols, width), BF16)

    for side, there_is in enumerate((above, below)):
        @pl.when(jnp.logical_not(there_is))
        def _():
            halo[side] = jnp.zeros((frames + 2, cols, width), BF16)

    for load in loads[4:]:
        load.wait()

    def inner(n, carry):
        l = frames - 1 - n
        for j in range(4):
            i = 4 * l + j - 4
            for t in range(0, rows, 2):
                a = jnp.concatenate([x[l + k, t:t + 2].reshape(2 * cols, width) for k in range(3)], axis=1)
                up[i, t * cols:(t + 2) * cols, :] = activation(a, j, tw, tb)
            for p in range(rows // 2 - 1):
                row = lambda q: up[i, pl.ds((2 * p + q) * cols, cols), :]
                for h, value in enumerate(row_pair(row, cols, w01, w2, left, mid, right, sb, p)):
                    out_ref[i, 2 * p + 1 + h] = value
        return carry

    def rim(n, carry):
        l = frames - 1 - n

        def temporal(j):
            a = jnp.concatenate([halo[:, l + k].reshape(2 * cols, width) for k in range(3)], axis=1)
            act = activation(a, j, tw, tb)
            zero = jnp.zeros((cols, width), BF16)
            edge[j][:cols] = jnp.where(above, act[:cols], zero)
            edge[j][cols:] = jnp.where(below, act[cols:], zero)

        def spatial(j):
            i = 4 * l + j - 4
            row = lambda h: up[i, pl.ds(h * cols, cols), :]
            first = [edge[j][:cols], row(0), row(1)]
            final = [row(rows - 2), row(rows - 1), edge[j][cols:]]
            a = jnp.concatenate([jnp.concatenate(first, axis=1), jnp.concatenate(final, axis=1)], axis=0)
            r = jnp.dot(a, w3[...], preferred_element_type=F32)
            for h in range(2):
                part = r[h * cols:(h + 1) * cols]
                left[2 * j + h, 8:8 + cols, :] = part[:, :wide]
                right[2 * j + h, 0:cols, :] = part[:, 2 * wide:]
                here = part[:, wide:2 * wide] + sb[...]
                total = pltpu.roll(left[2 * j + h], 1, 0)[8:] + here + pltpu.roll(right[2 * j + h], cols + 7, 0)[:cols]
                out_ref[i, h * (rows - 1)] = total.astype(BF16)

        temporal(0)
        temporal(1)
        spatial(0)
        temporal(2)
        spatial(1)
        temporal(3)
        spatial(2)
        spatial(3)
        return carry

    lax.fori_loop(0, frames - 2, inner, 0)
    arrived(2)
    inner(frames - 2, 0)
    arrived(0, 1)
    start(4, 5, 6, 7)
    lax.fori_loop(0, frames - 2, rim, 0)
    arrived(4, 5)
    rim(frames - 2, 0)
    arrived(3, 6, 7)

    for i in range(len(SENDS)):
        @pl.when(sends[i])
        def _():
            sent(i).wait_send()


def frames_call(sizes, latent, tw, tb, sw, sb):
    frames, rows, cols, width = latent.shape
    wide = sw.shape[3]
    vmem = pl.BlockSpec(memory_space=pltpu.VMEM)
    hbm = pl.BlockSpec(memory_space=pl.ANY)
    out_shape = [
        pltpu.VMEM((4 * frames - 3, rows, cols, wide), BF16),
        pltpu.VMEM((frames + 2, rows, cols, width), BF16),
        pltpu.VMEM((2, frames + 2, cols, width), BF16),
        pltpu.VMEM(tw.shape, BF16),
        pltpu.VMEM(tb.shape, F32),
        pltpu.VMEM(sb.shape, F32),
        pltpu.VMEM((3 * width, 2 * wide), BF16),
        pltpu.VMEM((4 * width, 2 * wide), BF16),
    ]
    return pl.pallas_call(
        functools.partial(frames_kernel, sizes),
        in_specs=[hbm] * 5,
        out_specs=[vmem] * len(out_shape),
        out_shape=out_shape,
        scratch_shapes=[
            pltpu.VMEM((4 * frames - 4, rows * cols, width), BF16),
            [pltpu.VMEM((2 * cols, width), BF16)] * 4,
            pltpu.VMEM(sw.shape, BF16),
            pltpu.VMEM((3 * width, 3 * wide), BF16),
            pltpu.VMEM((rows, cols + 8, wide), F32),
            pltpu.VMEM((rows, cols, wide), F32),
            pltpu.VMEM((rows, cols + 8, wide), F32),
            pltpu.SemaphoreType.DMA((frames + 4,)),
            pltpu.SemaphoreType.DMA((len(SENDS),)),
            pltpu.SemaphoreType.DMA((len(SENDS),)),
        ],
        compiler_params=pltpu.CompilerParams(
            collective_id=0, has_side_effects=True, vmem_limit_bytes=LIMIT
        ),
        cost_estimate=pl.CostEstimate(flops=28 * 10**9, bytes_accessed=16 * 10**6, transcendentals=10**7),
        name="frames",
    )(latent, tw, tb, sw, sb)


def finish_kernel(counts_ref, late_ref, x, halo, tw, tb, sb, w01, w2, out_ref,
                  early, up, left, mid, right, sem):
    rows, cols, width = x.shape[1:]
    fg, sp = lax.axis_index("fg"), lax.axis_index("sp")
    last_sp = lax.axis_size("sp") - 1
    limit = counts_ref[fg]

    def copy(source, f):
        return pltpu.make_async_copy(source, out_ref.at[f], sem)

    late = late_ref.shape[0] - 1
    for f in range(late):
        copy(late_ref.at[jnp.where(4 + f < limit, f, late)], 4 + f).start()
    early[4] = jnp.zeros(early.shape[1:], BF16)
    zero_rims(left, right, cols)

    def rows_of(t, k):
        if t == 0:
            return jnp.concatenate([halo[0, k], x[k, 0]], axis=0)
        if t == rows:
            return jnp.concatenate([x[k, rows - 1], halo[1, k]], axis=0)
        return x[k, t - 1:t + 1].reshape(2 * cols, width)

    for j in range(4):
        for t in range(0, rows + 2, 2):
            a = jnp.concatenate([rows_of(t, k) for k in range(3)], axis=1)
            act = activation(a, j, tw, tb)
            none = jnp.zeros((cols, width), BF16)
            first = jnp.where(sp > 0, act[:cols], none) if t == 0 else act[:cols]
            second = jnp.where(sp < last_sp, act[cols:], none) if t == rows else act[cols:]
            up[j, t * cols:(t + 1) * cols, :] = first
            up[j, (t + 1) * cols:(t + 2) * cols, :] = second

        for p in range(rows // 2):
            row = lambda q: up[j, pl.ds((2 * p + q) * cols, cols), :]
            for h, value in enumerate(row_pair(row, cols, w01, w2, left, mid, right, sb, p)):
                early[j, 2 * p + h] = value
        copy(early.at[jnp.where(j < limit, j, 4)], j).start()

    pltpu.make_async_copy(out_ref, out_ref, sem).wait()


def finish_call(counts, late, x, *args):
    _, rows, cols, wide = late.shape
    width = x.shape[3]
    shape = (late.shape[0] + 3, rows, cols, wide)
    vmem = pl.BlockSpec(memory_space=pltpu.VMEM)
    return pl.pallas_call(
        finish_kernel,
        in_specs=[pl.BlockSpec(memory_space=pltpu.SMEM)] + [vmem] * (2 + len(args)),
        out_specs=pl.BlockSpec(memory_space=pl.ANY),
        out_shape=jax.ShapeDtypeStruct(shape, BF16),
        scratch_shapes=[
            pltpu.VMEM((5,) + shape[1:], BF16),
            pltpu.VMEM((4, (rows + 2) * cols, width), BF16),
            pltpu.VMEM((rows, cols + 8, wide), F32),
            pltpu.VMEM((rows, cols, wide), F32),
            pltpu.VMEM((rows, cols + 8, wide), F32),
            pltpu.SemaphoreType.DMA(()),
        ],
        compiler_params=pltpu.CompilerParams(vmem_limit_bytes=24 * 1024 * 1024),
        cost_estimate=pl.CostEstimate(flops=9 * 10**9, bytes_accessed=16 * 10**6, transcendentals=10**6),
        name="finish",
    )(counts, late, x, *args)


def on_device(sizes, latent, temporal_weight, temporal_bias, spatial_weight, spatial_bias, counts):
    width = latent.shape[3]
    tw = temporal_weight.reshape(3 * width, 4 * width)
    args = (tw, temporal_bias.reshape(1, -1), spatial_weight, spatial_bias.reshape(1, -1))
    return finish_call(counts, *frames_call(sizes, latent, *args))


def solution(mesh):
    sizes = (mesh.shape["fg"], mesh.shape["sp"])
    return jax.shard_map(
        functools.partial(on_device, sizes),
        mesh=mesh,
        in_specs=(P("fg", "sp", None, None), P(), P(), P(), P(), P()),
        out_specs=P("fg", "sp", None, None),
        check_vma=False,
    )
```
